32 devices in a mesh: seq: 8 (over y, x, core), tp: 4 (over z).
Axes of the slice: x: 2, y: 2, z: 4, core: 2. Of those that a mesh axis runs over, the one named last changes fastest.
Arguments:
- tokens: bfloat16 [256, 8, 1152], P(None, 'seq'), may hold values from -6 to 6
- grad_out: bfloat16 [256, 8, 1152], P('seq'), may hold values from -6 to 6
- qkv_weight: bfloat16 [2, 1152, 3, 1152], P(None, None, None, 'tp'), may hold values from -1 to 1
- out_weight: bfloat16 [2, 1152, 1152], P(None, 'tp'), may hold values from -0.1875 to 0.1875
- mod_shift: float32 [2, 1152], replicated, may hold values from -3 to 3
- mod_scale: float32 [2, 1152], replicated, may hold values from -1.8 to 1.8
- mod_gate: float32 [2, 1152], replicated, may hold values from 0.5 to 1.5
Outputs:
- result: bfloat16 [256, 8, 1152], P('seq')
- grad_in: bfloat16 [256, 8, 1152], P(None, 'seq')
The draws below stay inside these ranges and needn't reach their ends.
All inputs are finite; a program needn't handle non-finite values.
Results may differ from the reference program's by a relative error of at most 0.035.
Values may be sent and summed in bfloat16 or wider, within the bound.
A program may use at most 64 MiB of HBM per device.

```python
import math
import jax
import jax.numpy as jnp
from jax import lax

HEADS = 16
HEAD_DIM = 72
D = 1152
P_SIZE = 256
FRAMES = 8
N_TP = 4


def draw_qkv_weight(key, part):
    key = jax.random.fold_in(key, 11)
    first = jax.random.fold_in(key, 0)
    base = jax.random.normal(first, (2, D, 3, D), jnp.float32) * D ** (-0.5)
    return jnp.clip(base, -1.0, 1.0).astype(jnp.bfloat16)


def steps_of(own_key, dims, cuts, smallest, top_value):
    loudness, own = 1.0, jax.random.fold_in(own_key, 6)
    for axis_at, parts in cuts:
        draws = jnp.exp(jax.random.uniform(jax.random.fold_in(own, axis_at), (parts,), jnp.float32, smallest / len(cuts), top_value / len(cuts)))
        loudness = loudness * jnp.repeat(draws, dims[axis_at] // parts).reshape([-1 if axis == axis_at else 1 for axis in range(len(dims))])
    return loudness


def scatter_about(own_key, extent, width, bound, cuts=(), dtype=jnp.bfloat16):
    entries = jax.random.normal(own_key, extent, jnp.float32) * width
    if len(cuts) > 0:
        entries = steps_of(own_key, extent, cuts, -0.22, 0.18) * entries
    return jnp.clip(entries, min=-bound, max=bound).astype(dtype)


def setup_inputs(seed: int = 0) -> dict:
    key_of = jax.random.split(jax.random.key(seed), 8)
    return {
        "tokens": scatter_about(key_of[0], (P_SIZE, FRAMES, D), 1.0, 6.0, ((1, 8),)),
        "grad_out": scatter_about(key_of[1], (P_SIZE, FRAMES, D), 1.0, 6.0, ((0, 8),)),
        "qkv_weight": draw_qkv_weight(jax.random.fold_in(key_of[7], 71), 0),
        "out_weight": scatter_about(key_of[3], (2, D, D), D ** -0.5, 0.1875, ((1, 4),)),
        "mod_shift": scatter_about(key_of[4], (2, D), 0.5, 3.0, (), jnp.float32),
        "mod_scale": scatter_about(key_of[5], (2, D), 0.3, 1.8, (), jnp.float32),
        "mod_gate": jnp.clip(jax.random.uniform(key_of[6], (2, D), jnp.float32, 0.5, 1.5), 0.5, 1.5),
    }


def rounded(value):
    return lax.optimization_barrier(value.astype(jnp.bfloat16))

def normalize(tokens, shift_row, scale_row):
    widened = tokens.astype(jnp.float32)
    center = widened - lax.optimization_barrier(jnp.mean(widened, axis=-1, keepdims=True))
    inv_std = lax.rsqrt(lax.optimization_barrier(jnp.mean(center * center, axis=-1, keepdims=True)) + 1e-06)
    normed = center * inv_std
    modded = rounded(normed * (1.0 + scale_row) + shift_row)
    return (modded, normed, inv_std)

def sequence_probs(queries, key_heads):
    scores = jnp.einsum('lhe,mhe->hlm', queries.astype(jnp.float32), key_heads.astype(jnp.float32)) / math.sqrt(HEAD_DIM)
    probs_high = jax.nn.softmax(scores, axis=-1)
    return (probs_high, rounded(probs_high))

def sequence_forward(group_in):
    queries, key_heads, value_heads = group_in
    probs_high, probs_low = sequence_probs(queries, key_heads)
    attended = jnp.einsum('hlm,mhe->lhe', probs_low.astype(jnp.float32), value_heads.astype(jnp.float32))
    return rounded(attended)

def sequence_backward(group_in):
    queries, key_heads, value_heads, grad_attn = group_in
    probs_high, probs_low = sequence_probs(queries, key_heads)
    grad_probs = jnp.einsum('lhe,mhe->hlm', grad_attn.astype(jnp.float32), value_heads.astype(jnp.float32))
    grad_scores = rounded(probs_high * (grad_probs - lax.optimization_barrier(jnp.sum(probs_high * grad_probs, axis=-1, keepdims=True))) / math.sqrt(HEAD_DIM))
    grad_query = rounded(jnp.einsum('hlm,mhe->lhe', grad_scores.astype(jnp.float32), key_heads.astype(jnp.float32)))
    grad_keys = rounded(jnp.einsum('hlm,lhe->mhe', grad_scores.astype(jnp.float32), queries.astype(jnp.float32)))
    grad_values = rounded(jnp.einsum('hlm,lhe->mhe', probs_low.astype(jnp.float32), grad_attn.astype(jnp.float32)))
    return (grad_query, grad_keys, grad_values)

def heads_of(tokens, in_weight, shift_row, scale_row):
    modded, normed, inv_std = normalize(tokens, shift_row, scale_row)
    projected = rounded(jnp.dot(modded.reshape(-1, D), in_weight.reshape(D, 3 * D), preferred_element_type=jnp.float32))
    projected = projected.reshape(tokens.shape[0], tokens.shape[1], 3, HEADS, HEAD_DIM)
    return (projected[:, :, 0], projected[:, :, 1], projected[:, :, 2], normed, inv_std)

def run_forward(queries, key_heads, value_heads, spatial):
    if spatial:
        moved = tuple((jnp.swapaxes(item, 0, 1) for item in (queries, key_heads, value_heads)))
        return jnp.swapaxes(lax.map(sequence_forward, moved), 0, 1)
    return lax.map(sequence_forward, (queries, key_heads, value_heads))

def run_backward(queries, key_heads, value_heads, grad_attn, spatial):
    if spatial:
        moved = tuple((jnp.swapaxes(item, 0, 1) for item in (queries, key_heads, value_heads, grad_attn)))
        outputs = lax.map(sequence_backward, moved)
        return tuple((jnp.swapaxes(item, 0, 1) for item in outputs))
    return lax.map(sequence_backward, (queries, key_heads, value_heads, grad_attn))

def block_forward(tokens, in_weight, out_matrix, shift_row, scale_row, gate_row, spatial):
    queries, key_heads, value_heads, normed, inv_std = heads_of(tokens, in_weight, shift_row, scale_row)
    attended = run_forward(queries, key_heads, value_heads, spatial).reshape(-1, D)
    group_width = D // N_TP
    total = jnp.zeros((attended.shape[0], D), jnp.float32)
    for group in range(N_TP):
        lower = group * group_width
        piece = jnp.dot(attended[:, lower:lower + group_width], out_matrix[lower:lower + group_width, :], preferred_element_type=jnp.float32)
        total = total + rounded(piece).astype(jnp.float32)
    return (tokens.astype(jnp.float32) + gate_row * total.reshape(tokens.shape)).astype(jnp.bfloat16)

def block_backward(tokens, grad, in_weight, out_matrix, shift_row, scale_row, gate_row, spatial):
    queries, key_heads, value_heads, normed, inv_std = heads_of(tokens, in_weight, shift_row, scale_row)
    grad_proj = rounded(gate_row * grad.astype(jnp.float32))
    grad_attn = rounded(jnp.dot(grad_proj.reshape(-1, D), out_matrix.T, preferred_element_type=jnp.float32))
    grad_attn = grad_attn.reshape(queries.shape)
    grad_query, grad_keys, grad_values = run_backward(queries, key_heads, value_heads, grad_attn, spatial)
    stacked = jnp.stack([grad_query, grad_keys, grad_values], axis=2).reshape(-1, 3, D)
    group_width = D // N_TP
    total = jnp.zeros((stacked.shape[0], D), jnp.float32)
    for group in range(N_TP):
        lower = group * group_width
        picked = stacked[:, :, lower:lower + group_width].reshape(-1, 3 * group_width)
        columns = in_weight[:, :, lower:lower + group_width].reshape(D, 3 * group_width)
        piece = jnp.dot(picked, columns.T, preferred_element_type=jnp.float32)
        total = total + rounded(piece).astype(jnp.float32)
    grad_norm = total.reshape(tokens.shape) * (1.0 + scale_row)
    back_part = inv_std * (grad_norm - lax.optimization_barrier(jnp.mean(grad_norm, axis=-1, keepdims=True)) - normed * lax.optimization_barrier(jnp.mean(grad_norm * normed, axis=-1, keepdims=True)))
    return (grad.astype(jnp.float32) + back_part).astype(jnp.bfloat16)

def reference(tokens, grad_out, qkv_weight, out_weight, mod_shift, mod_scale, mod_gate):
    middle = block_forward(tokens, qkv_weight[0], out_weight[0], mod_shift[0], mod_scale[0], mod_gate[0], True)
    result = block_forward(middle, qkv_weight[1], out_weight[1], mod_shift[1], mod_scale[1], mod_gate[1], False)
    grad_mid = block_backward(middle, grad_out, qkv_weight[1], out_weight[1], mod_shift[1], mod_scale[1], mod_gate[1], False)
    grad_in = block_backward(tokens, grad_mid, qkv_weight[0], out_weight[0], mod_shift[0], mod_scale[0], mod_gate[0], True)
    return (result, grad_in)
```

```python
import functools
import math

import jax
import jax.numpy as jnp
from jax import lax
from jax.experimental import pallas as pl
from jax.experimental.pallas import tpu as pltpu
from jax.sharding import PartitionSpec as P

HEAD_DIM = 72
BF16 = jnp.bfloat16
F32 = jnp.float32
MESH = pl.DeviceIdType.MESH
VMEM = pl.BlockSpec(memory_space=pltpu.VMEM)
LIMIT = 48 * 1024 * 1024


def dot_nn(a, b):
    return lax.dot_general(a, b, (((1,), (0,)), ((), ())), preferred_element_type=F32)


def dot_nt(a, b):
    return lax.dot_general(a, b, (((1,), (1,)), ((), ())), preferred_element_type=F32)


def dot_tn(a, b):
    return lax.dot_general(a, b, (((0,), (0,)), ((), ())), preferred_element_type=F32)


def normalize(rows):
    widened = rows.astype(F32)
    center = widened - jnp.mean(widened, axis=-1, keepdims=True)
    inv_std = lax.rsqrt(jnp.mean(center * center, axis=-1, keepdims=True) + 1e-06)
    return center * inv_std, inv_std


def project(rows, shift_ref, scale_ref, weight_ref):
    normed, _ = normalize(rows)
    modded = (normed * (1.0 + scale_ref[...]) + shift_ref[...]).astype(BF16)
    return tuple(dot_nn(modded, weight_ref[c]).astype(BF16) for c in range(3))


def head_masks(width):
    lane = lax.broadcasted_iota(jnp.int32, (1, width), 1)
    return [
        (lane >= h * HEAD_DIM) & (lane < (h + 1) * HEAD_DIM) for h in range(width // HEAD_DIM)
    ]


def pick(mask, value):
    return jnp.where(mask, value, jnp.zeros_like(value))


def head_probs(queries, keys, mask, same):
    scores = dot_nt(pick(mask, queries), keys) * (1.0 / math.sqrt(HEAD_DIM))
    if same is not None:
        scores = jnp.where(same, scores, -jnp.inf)
    shifted = jnp.exp(scores - jnp.max(scores, axis=-1, keepdims=True))
    return shifted / jnp.sum(shifted, axis=-1, keepdims=True)


def same_patch(total, seqs, part):
    row = lax.broadcasted_iota(jnp.int32, (total, total), 0)
    col = lax.broadcasted_iota(jnp.int32, (total, total), 1)
    block = seqs * part
    return (row // block == col // block) & (row % part == col % part)


def backward_heads(queries, keys, values, grad_attn, probs_of):
    masks = head_masks(queries.shape[1])
    grads = [jnp.zeros(queries.shape, F32) for _ in range(3)]
    for h, mask in enumerate(masks):
        probs = probs_of(h, mask)
        grad_probs = dot_nt(pick(mask, grad_attn), values)
        mean = jnp.sum(probs * grad_probs, axis=-1, keepdims=True)
        grad_scores = (probs * (grad_probs - mean) * (1.0 / math.sqrt(HEAD_DIM))).astype(BF16)
        grads[0] = jnp.where(mask, dot_nn(grad_scores, keys), grads[0])
        grads[1] = jnp.where(mask, dot_tn(grad_scores, queries), grads[1])
        grads[2] = jnp.where(mask, dot_tn(probs.astype(BF16), grad_attn), grads[2])
    return [grad.astype(BF16) for grad in grads]


def back_project(grads, weight_ref):
    total = dot_nt(grads[0], weight_ref[0])
    total += dot_nt(grads[1], weight_ref[1])
    return total + dot_nt(grads[2], weight_ref[2])


def as_rows(ref):
    return ref[...].astype(F32).reshape(-1, ref.shape[-1])


def put(ref, value):
    ref[...] = value.reshape(ref.shape).astype(BF16)


def spatial_forward(x_ref, shift_ref, scale_ref, weight_ref, out_ref, part_ref, qkv_ref):
    queries, keys, values = project(as_rows(x_ref), shift_ref, scale_ref, weight_ref)
    attended = jnp.zeros(queries.shape, F32)
    for mask in head_masks(queries.shape[1]):
        probs = head_probs(queries, keys, mask, None).astype(BF16)
        attended = jnp.where(mask, dot_nn(probs, values), attended)
    put(part_ref, dot_nn(attended.astype(BF16), out_ref[...]))
    for c, item in enumerate((queries, keys, values)):
        qkv_ref[c] = item


def grad_of_attended(g_ref, gate_ref, out_ref):
    grad_proj = (gate_ref[...] * as_rows(g_ref)).astype(BF16)
    return dot_nt(grad_proj, out_ref[...]).astype(BF16)


def spatial_backward(g_ref, gate_ref, weight_ref, out_ref, qkv_ref, part_ref):
    queries, keys, values = (qkv_ref[c] for c in range(3))
    grad_attn = grad_of_attended(g_ref, gate_ref, out_ref)
    grads = backward_heads(
        queries, keys, values, grad_attn, lambda h, mask: head_probs(queries, keys, mask, None)
    )
    put(part_ref, back_project(grads, weight_ref))


def temporal(
    x_ref, g_ref, shift_ref, scale_ref, gate_ref, weight_ref, out_ref, part_ref, gpart_ref
):
    _, seqs, part, _ = x_ref.shape
    queries, keys, values = project(as_rows(x_ref), shift_ref, scale_ref, weight_ref)
    same = same_patch(queries.shape[0], seqs, part)
    grad_attn = grad_of_attended(g_ref, gate_ref, out_ref)
    probs = []
    attended = jnp.zeros(queries.shape, F32)
    for mask in head_masks(queries.shape[1]):
        probs.append(head_probs(queries, keys, mask, same))
        attended = jnp.where(mask, dot_nn(probs[-1].astype(BF16), values), attended)
    put(part_ref, dot_nn(attended.astype(BF16), out_ref[...]))
    grads = backward_heads(queries, keys, values, grad_attn, lambda h, mask: probs[h])
    put(gpart_ref, back_project(grads, weight_ref))


def forward_end(total, x_ref, c, gate_ref):
    return (x_ref[c].astype(F32) + gate_ref[...] * total).astype(BF16)


def backward_end(total, x_ref, c, g_ref, scale_ref):
    normed, inv_std = normalize(x_ref[c])
    grad_norm = total * (1.0 + scale_ref[...])
    back = inv_std * (
        grad_norm
        - jnp.mean(grad_norm, axis=-1, keepdims=True)
        - normed * jnp.mean(grad_norm * normed, axis=-1, keepdims=True)
    )
    return (g_ref[c].astype(F32) + back).astype(BF16)


def head_sums(parts, totals, ends, moved, scratch, seqs, tps):
    inbox, halves, others, sems, seq_sems, own_sem = scratch
    s, z = lax.axis_index("seq"), lax.axis_index("tp")
    chunks = parts[0].shape[0]
    inner = (z > 0) & (z < tps - 1)
    outer = jnp.logical_not(inner)
    near = jnp.where(z < tps // 2, z + 1, z - 1)
    far = jnp.where(z < tps // 2, z - 1, z + 1)
    across = near
    barrier = pltpu.get_barrier_semaphore()

    def greet(tp):
        pl.semaphore_signal(barrier, inc=1, device_id=(s, tp), device_id_type=MESH)

    greet(near)

    @pl.when(inner)
    def _():
        greet(far)

    any_moved = any(item is not None for item in moved)
    if any_moved:

        @pl.loop(1, seqs)
        def _(k):
            pl.semaphore_signal(
                barrier, inc=1, device_id=(lax.rem(s + k, seqs), z), device_id_type=MESH
            )

    peers = seqs - 1 if any_moved else 0

    @pl.when(inner)
    def _():
        pl.semaphore_wait(barrier, 2 + peers)

    @pl.when(outer)
    def _():
        pl.semaphore_wait(barrier, 1 + peers)

    items = [(i, c) for c in range(chunks) for i in range(len(parts))]

    def remote(src, dst, kind, i, c, tp):
        return pltpu.make_async_remote_copy(
            src_ref=src.at[c],
            dst_ref=dst.at[c],
            send_sem=sems.at[kind, 0, i, c],
            recv_sem=sems.at[kind, 1, i, c],
            device_id=(s, tp),
            device_id_type=MESH,
        )

    def inward(i, c):
        return remote(parts[i], inbox.at[i], 0, i, c, near)

    def cross(i, c):
        return remote(halves.at[i], others.at[i], 1, i, c, across)

    def outward(i, c):
        return remote(totals[i], totals[i], 2, i, c, far)

    def spread(i, c):
        @pl.loop(1, seqs)
        def _(k):
            to = lax.rem(s + k, seqs)
            pltpu.make_async_remote_copy(
                src_ref=totals[i].at[c, to],
                dst_ref=moved[i].at[c, s],
                send_sem=seq_sems.at[0, c],
                recv_sem=seq_sems.at[1, c],
                device_id=(to, z),
                device_id_type=MESH,
            ).start()

        pltpu.make_async_copy(totals[i].at[c, s], moved[i].at[c, s], own_sem.at[c]).start()

    @pl.when(outer)
    def _():
        for i, c in items:
            inward(i, c).start()
        for i, c in items:
            outward(i, c).wait_recv()
            if moved[i] is not None:
                spread(i, c)
        for i, c in items:
            inward(i, c).wait_send()

    @pl.when(inner)
    def _():
        def fold(i, c):
            inward(i, c).wait_recv()
            halves[i, c] = (parts[i][c].astype(F32) + inbox[i, c].astype(F32)).astype(BF16)
            cross(i, c).start()

        def finish(i, c):
            cross(i, c).wait_recv()
            total = halves[i, c].astype(F32) + others[i, c].astype(F32)
            totals[i][c] = ends[i](total, c)
            outward(i, c).start()
            if moved[i] is not None:
                spread(i, c)

        lead = 2
        for at in range(len(items) + lead):
            if at < len(items):
                fold(*items[at])
            if at >= lead:
                finish(*items[at - lead])
        for i, c in items:
            cross(i, c).wait_send()
            outward(i, c).wait_send()

    for i, c in items:
        if moved[i] is not None:
            pltpu.make_async_copy(totals[i].at[c, s], moved[i].at[c, s], own_sem.at[c]).wait()
            rest = pl.ds(0, seqs - 1)
            both = pltpu.make_async_remote_copy(
                src_ref=totals[i].at[c, rest],
                dst_ref=moved[i].at[c, rest],
                send_sem=seq_sems.at[0, c],
                recv_sem=seq_sems.at[1, c],
                device_id=(lax.rem(s + 1, seqs), z),
                device_id_type=MESH,
            )
            both.wait_send()
            both.wait_recv()


def middle_kernel(seqs, tps, part_ref, x_ref, gate_ref, mid_ref, total, *scratch):
    ends = [lambda value, c: forward_end(value, x_ref, c, gate_ref)]
    head_sums([part_ref], [total], ends, [mid_ref], scratch, seqs, tps)


def temporal_sums(
    seqs, tps, gpart_ref, part_ref, x_ref, g_ref, gate_ref, scale_ref, result_ref, back_ref,
    total, *scratch
):
    ends = [
        lambda value, c: backward_end(value, x_ref, c, g_ref, scale_ref),
        lambda value, c: forward_end(value, x_ref, c, gate_ref),
    ]
    head_sums(
        [gpart_ref, part_ref], [total, result_ref], ends, [back_ref, None], scratch, seqs, tps
    )


def spatial_sums(seqs, tps, gpart_ref, x_ref, g_ref, scale_ref, grad_ref, *scratch):
    ends = [lambda value, c: backward_end(value, x_ref, c, g_ref, scale_ref)]
    head_sums([gpart_ref], [grad_ref], ends, [None], scratch, seqs, tps)


def compute(body, outs, *operands):
    return pl.pallas_call(
        body,
        out_shape=outs,
        in_specs=[VMEM] * len(operands),
        out_specs=jax.tree.map(lambda _: VMEM, outs),
        compiler_params=pltpu.CompilerParams(vmem_limit_bytes=LIMIT),
    )(*operands)


def exchange(body, ident, outs, streams, own_total, seqs, tps, *operands):
    shape = operands[0].shape
    chunks = shape[0]
    scratch = [pltpu.VMEM(shape, BF16)] if own_total else []
    scratch += [pltpu.VMEM((streams, *shape), BF16)] * 3
    scratch += [
        pltpu.SemaphoreType.DMA((3, 2, streams, chunks)),
        pltpu.SemaphoreType.DMA((2, chunks)),
        pltpu.SemaphoreType.DMA((chunks,)),
    ]
    return pl.pallas_call(
        functools.partial(body, seqs, tps),
        out_shape=outs,
        in_specs=[VMEM] * len(operands),
        out_specs=jax.tree.map(lambda _: VMEM, outs),
        scratch_shapes=scratch,
        compiler_params=pltpu.CompilerParams(
            collective_id=ident, has_side_effects=True, vmem_limit_bytes=LIMIT
        ),
    )(*operands)


def per_device(
    seqs, tps, tokens, grad_out, qkv_weight, out_weight, mod_shift, mod_scale, mod_gate
):
    width = tokens.shape[-1]
    patches = tokens.shape[0] // seqs
    chunks = max(1, patches // 8)
    part = patches // chunks
    dims = (chunks, seqs, part, width)
    array = jax.ShapeDtypeStruct(dims, BF16)
    weights = jnp.transpose(qkv_weight, (0, 2, 1, 3))
    rows = [[item[b : b + 1] for b in range(2)] for item in (mod_shift, mod_scale, mod_gate)]
    shift, scale, gate = rows
    x = tokens.reshape(seqs, chunks, part, width).transpose(1, 0, 2, 3)
    g = grad_out.reshape(chunks, part, seqs, width).transpose(0, 2, 1, 3)

    cached = jax.ShapeDtypeStruct((3, tokens.shape[0], out_weight.shape[1]), BF16)
    part_s, qkv_s = compute(
        spatial_forward, (array, cached), x, shift[0], scale[0], weights[0], out_weight[0]
    )
    mid = exchange(middle_kernel, 0, array, 1, True, seqs, tps, part_s, x, gate[0])
    part_t, gpart_t = compute(
        temporal, (array, array), mid, g, shift[1], scale[1], gate[1], weights[1], out_weight[1]
    )
    result, grad_mid = exchange(
        temporal_sums, 1, (array, array), 2, True, seqs, tps,
        gpart_t, part_t, mid, g, gate[1], scale[1],
    )
    gpart_s = compute(
        spatial_backward, array, grad_mid, gate[0], weights[0], out_weight[0], qkv_s
    )
    grad_in = exchange(spatial_sums, 2, array, 1, False, seqs, tps, gpart_s, x, grad_mid, scale[0])
    result = result.transpose(0, 2, 1, 3).reshape(grad_out.shape)
    return (result, grad_in.transpose(1, 0, 2, 3).reshape(tokens.shape))


def solution(mesh):
    in_specs = (
        P(None, "seq", None),
        P("seq", None, None),
        P(None, None, None, "tp"),
        P(None, "tp", None),
        P(),
        P(),
        P(),
    )
    out_specs = (P("seq", None, None), P(None, "seq", None))
    return jax.shard_map(
        functools.partial(per_device, mesh.shape["seq"], mesh.shape["tp"]),
        mesh=mesh,
        in_specs=in_specs,
        out_specs=out_specs,
        check_vma=False,
    )
```

```python
import functools
import math

import jax
import jax.numpy as jnp
from jax import lax
from jax.experimental import pallas as pl
from jax.experimental.pallas import tpu as pltpu
from jax.sharding import PartitionSpec as P

HEAD_DIM = 72
BF16 = jnp.bfloat16
F32 = jnp.float32
MESH = pl.DeviceIdType.MESH
VMEM = pl.BlockSpec(memory_space=pltpu.VMEM)
LIMIT = 48 * 1024 * 1024


def dot_nn(a, b):
    return lax.dot_general(a, b, (((1,), (0,)), ((), ())), preferred_element_type=F32)


def dot_nt(a, b):
    return lax.dot_general(a, b, (((1,), (1,)), ((), ())), preferred_element_type=F32)


def dot_tn(a, b):
    return lax.dot_general(a, b, (((0,), (0,)), ((), ())), preferred_element_type=F32)


def normalize(rows):
    widened = rows.astype(F32)
    center = widened - jnp.mean(widened, axis=-1, keepdims=True)
    inv_std = lax.rsqrt(jnp.mean(center * center, axis=-1, keepdims=True) + 1e-06)
    return center * inv_std, inv_std


def project(rows, shift_ref, scale_ref, weight_ref, b):
    normed, _ = normalize(rows)
    modded = (normed * (1.0 + scale_ref[b : b + 1]) + shift_ref[b : b + 1]).astype(BF16)
    return tuple(dot_nn(modded, weight_ref[b, c]).astype(BF16) for c in range(3))


def head_masks(width):
    lane = lax.broadcasted_iota(jnp.int32, (1, width), 1)
    return [
        (lane >= h * HEAD_DIM) & (lane < (h + 1) * HEAD_DIM) for h in range(width // HEAD_DIM)
    ]


def pick(mask, value):
    return jnp.where(mask, value, jnp.zeros_like(value))


def head_probs(queries, keys, mask, same):
    scores = dot_nt(pick(mask, queries), keys) * (1.0 / math.sqrt(HEAD_DIM))
    if same is not None:
        scores = jnp.where(same, scores, -jnp.inf)
    shifted = jnp.exp(scores - jnp.max(scores, axis=-1, keepdims=True))
    return shifted / jnp.sum(shifted, axis=-1, keepdims=True)


def same_patch(total, seqs, part):
    row = lax.broadcasted_iota(jnp.int32, (total, total), 0)
    col = lax.broadcasted_iota(jnp.int32, (total, total), 1)
    block = seqs * part
    return (row // block == col // block) & (row % part == col % part)


def backward_heads(queries, keys, values, grad_attn, probs_of):
    masks = head_masks(queries.shape[1])
    grads = [jnp.zeros(queries.shape, F32) for _ in range(3)]
    for h, mask in enumerate(masks):
        probs = probs_of(h, mask)
        grad_probs = dot_nt(pick(mask, grad_attn), values)
        mean = jnp.sum(probs * grad_probs, axis=-1, keepdims=True)
        grad_scores = (probs * (grad_probs - mean) * (1.0 / math.sqrt(HEAD_DIM))).astype(BF16)
        grads[0] = jnp.where(mask, dot_nn(grad_scores, keys), grads[0])
        grads[1] = jnp.where(mask, dot_tn(grad_scores, queries), grads[1])
        grads[2] = jnp.where(mask, dot_tn(probs.astype(BF16), grad_attn), grads[2])
    return [grad.astype(BF16) for grad in grads]


def back_project(grads, weight_ref, b):
    total = dot_nt(grads[0], weight_ref[b, 0])
    total += dot_nt(grads[1], weight_ref[b, 1])
    return total + dot_nt(grads[2], weight_ref[b, 2])


def as_rows(ref):
    return ref[...].astype(F32).reshape(-1, ref.shape[-1])


def put(ref, value):
    ref[...] = value.reshape(ref.shape).astype(BF16)


def spatial_forward(x_ref, shift_ref, scale_ref, weight_ref, out_ref, part_ref, qkv_ref):
    queries, keys, values = project(as_rows(x_ref), shift_ref, scale_ref, weight_ref, 0)
    attended = jnp.zeros(queries.shape, F32)
    for mask in head_masks(queries.shape[1]):
        probs = head_probs(queries, keys, mask, None).astype(BF16)
        attended = jnp.where(mask, dot_nn(probs, values), attended)
    put(part_ref, dot_nn(attended.astype(BF16), out_ref[0]))
    for c, item in enumerate((queries, keys, values)):
        qkv_ref[c] = item


def grad_of_attended(g_ref, gate_ref, out_ref, b):
    grad_proj = (gate_ref[b : b + 1] * as_rows(g_ref)).astype(BF16)
    return dot_nt(grad_proj, out_ref[b]).astype(BF16)


def spatial_backward(g_ref, gate_ref, weight_ref, out_ref, qkv_ref, part_ref):
    queries, keys, values = (qkv_ref[c] for c in range(3))
    grad_attn = grad_of_attended(g_ref, gate_ref, out_ref, 0)
    grads = backward_heads(
        queries, keys, values, grad_attn, lambda h, mask: head_probs(queries, keys, mask, None)
    )
    put(part_ref, back_project(grads, weight_ref, 0))


def temporal(
    x_ref, g_ref, shift_ref, scale_ref, gate_ref, weight_ref, out_ref, part_ref, gpart_ref
):
    _, seqs, part, _ = x_ref.shape
    queries, keys, values = project(as_rows(x_ref), shift_ref, scale_ref, weight_ref, 1)
    same = same_patch(queries.shape[0], seqs, part)
    grad_attn = grad_of_attended(g_ref, gate_ref, out_ref, 1)
    probs = []
    attended = jnp.zeros(queries.shape, F32)
    for mask in head_masks(queries.shape[1]):
        probs.append(head_probs(queries, keys, mask, same))
        attended = jnp.where(mask, dot_nn(probs[-1].astype(BF16), values), attended)
    put(part_ref, dot_nn(attended.astype(BF16), out_ref[1]))
    grads = backward_heads(queries, keys, values, grad_attn, lambda h, mask: probs[h])
    put(gpart_ref, back_project(grads, weight_ref, 1))


def forward_end(total, x_ref, piece, gate_ref, b):
    return (x_ref[piece].astype(F32) + gate_ref[b : b + 1] * total).astype(BF16)


def backward_end(total, x_ref, piece, g_ref, scale_ref, b):
    normed, inv_std = normalize(x_ref[piece])
    grad_norm = total * (1.0 + scale_ref[b : b + 1])
    back = inv_std * (
        grad_norm
        - jnp.mean(grad_norm, axis=-1, keepdims=True)
        - normed * jnp.mean(grad_norm * normed, axis=-1, keepdims=True)
    )
    return (g_ref[piece].astype(F32) + back).astype(BF16)


def head_sums(parts, totals, ends, moved, scratch, seqs, tps, splits):
    inbox, halves, others, sems, seq_sems, own_sem = scratch
    s, z = lax.axis_index("seq"), lax.axis_index("tp")
    chunks = parts[0].shape[0]
    inner = (z > 0) & (z < tps - 1)
    outer = jnp.logical_not(inner)
    near = jnp.where(z < tps // 2, z + 1, z - 1)
    far = jnp.where(z < tps // 2, z - 1, z + 1)
    across = near
    barrier = pltpu.get_barrier_semaphore()

    def greet(tp):
        pl.semaphore_signal(barrier, inc=1, device_id=(s, tp), device_id_type=MESH)

    greet(near)

    @pl.when(inner)
    def _():
        greet(far)

    any_moved = any(item is not None for item in moved)
    if any_moved:

        @pl.loop(1, seqs)
        def _(k):
            pl.semaphore_signal(
                barrier, inc=1, device_id=(lax.rem(s + k, seqs), z), device_id_type=MESH
            )

    peers = seqs - 1 if any_moved else 0

    @pl.when(inner)
    def _():
        pl.semaphore_wait(barrier, 2 + peers)

    @pl.when(outer)
    def _():
        pl.semaphore_wait(barrier, 1 + peers)

    step = seqs // splits
    items = [(i, k) for k in range(chunks * splits) for i in range(len(parts))]

    def piece_of(k):
        return k // splits, pl.ds(k % splits * step, step)

    def remote(src, dst, kind, i, k, tp):
        return pltpu.make_async_remote_copy(
            src_ref=src.at[piece_of(k)],
            dst_ref=dst.at[piece_of(k)],
            send_sem=sems.at[kind, 0, i, k],
            recv_sem=sems.at[kind, 1, i, k],
            device_id=(s, tp),
            device_id_type=MESH,
        )

    def inward(i, c):
        return remote(parts[i], inbox.at[i], 0, i, c, near)

    def cross(i, c):
        return remote(halves.at[i], others.at[i], 1, i, c, across)

    def outward(i, c):
        return remote(totals[i], totals[i], 2, i, c, far)

    def spread(i, k):
        c, first = k // splits, k % splits * step

        @pl.loop(first, first + step)
        def _(to):
            @pl.when(to != s)
            def _():
                pltpu.make_async_remote_copy(
                    src_ref=totals[i].at[c, to],
                    dst_ref=moved[i].at[c, s],
                    send_sem=seq_sems.at[0, c],
                    recv_sem=seq_sems.at[1, c],
                    device_id=(to, z),
                    device_id_type=MESH,
                ).start()

            @pl.when(to == s)
            def _():
                pltpu.make_async_copy(
                    totals[i].at[c, s], moved[i].at[c, s], own_sem.at[c]
                ).start()

    count = len(items)

    @pl.when(outer)
    def _():
        flight, lead = 4, 8
        for at in range(count + lead):
            if at < count:
                if at >= flight:
                    inward(*items[at - flight]).wait_send()
                inward(*items[at]).start()
            if at >= lead:
                i, k = items[at - lead]
                outward(i, k).wait_recv()
                if moved[i] is not None:
                    spread(i, k)
        for item in items[count - flight :]:
            inward(*item).wait_send()

    @pl.when(inner)
    def _():
        def fold(i, k):
            inward(i, k).wait_recv()
            at = (i, *piece_of(k))
            halves[at] = (parts[i][at[1:]].astype(F32) + inbox[at].astype(F32)).astype(BF16)
            cross(i, k).start()

        def finish(i, k):
            cross(i, k).wait_recv()
            at = (i, *piece_of(k))
            total = halves[at].astype(F32) + others[at].astype(F32)
            totals[i][at[1:]] = ends[i](total, at[1:])
            outward(i, k).start()
            if moved[i] is not None:
                spread(i, k)

        lead = 3
        for at in range(count + lead):
            if at < count:
                fold(*items[at])
            if at >= lead:
                finish(*items[at - lead])
        for i, k in items:
            cross(i, k).wait_send()
            outward(i, k).wait_send()

    for i, c in [(i, c) for c in range(chunks) for i in range(len(parts))]:
        if moved[i] is not None:
            pltpu.make_async_copy(totals[i].at[c, s], moved[i].at[c, s], own_sem.at[c]).wait()
            rest = pl.ds(0, seqs - 1)
            both = pltpu.make_async_remote_copy(
                src_ref=totals[i].at[c, rest],
                dst_ref=moved[i].at[c, rest],
                send_sem=seq_sems.at[0, c],
                recv_sem=seq_sems.at[1, c],
                device_id=(lax.rem(s + 1, seqs), z),
                device_id_type=MESH,
            )
            both.wait_send()
            both.wait_recv()


def middle_kernel(seqs, tps, splits, part_ref, x_ref, gate_ref, mid_ref, total, *scratch):
    ends = [lambda value, at: forward_end(value, x_ref, at, gate_ref, 0)]
    head_sums([part_ref], [total], ends, [mid_ref], scratch, seqs, tps, splits)


def temporal_sums(
    seqs, tps, splits, gpart_ref, part_ref, x_ref, g_ref, gate_ref, scale_ref, result_ref, back_ref,
    total, *scratch
):
    ends = [
        lambda value, at: backward_end(value, x_ref, at, g_ref, scale_ref, 1),
        lambda value, at: forward_end(value, x_ref, at, gate_ref, 1),
    ]
    head_sums(
        [gpart_ref, part_ref], [total, result_ref], ends, [back_ref, None],
        scratch, seqs, tps, splits,
    )


def spatial_sums(seqs, tps, splits, gpart_ref, x_ref, g_ref, scale_ref, grad_ref, *scratch):
    ends = [lambda value, at: backward_end(value, x_ref, at, g_ref, scale_ref, 0)]
    head_sums([gpart_ref], [grad_ref], ends, [None], scratch, seqs, tps, splits)


def compute(body, outs, *operands):
    return pl.pallas_call(
        body,
        out_shape=outs,
        in_specs=[VMEM] * len(operands),
        out_specs=jax.tree.map(lambda _: VMEM, outs),
        compiler_params=pltpu.CompilerParams(vmem_limit_bytes=LIMIT),
    )(*operands)


def exchange(body, ident, outs, streams, own_total, seqs, tps, splits, *operands):
    shape = operands[0].shape
    chunks = shape[0]
    splits = math.gcd(seqs, splits)
    scratch = [pltpu.VMEM(shape, BF16)] if own_total else []
    scratch += [pltpu.VMEM((streams, *shape), BF16)] * 3
    scratch += [
        pltpu.SemaphoreType.DMA((3, 2, streams, chunks * splits)),
        pltpu.SemaphoreType.DMA((2, chunks)),
        pltpu.SemaphoreType.DMA((chunks,)),
    ]
    return pl.pallas_call(
        functools.partial(body, seqs, tps, splits),
        out_shape=outs,
        in_specs=[VMEM] * len(operands),
        out_specs=jax.tree.map(lambda _: VMEM, outs),
        scratch_shapes=scratch,
        compiler_params=pltpu.CompilerParams(
            collective_id=ident, has_side_effects=True, vmem_limit_bytes=LIMIT
        ),
    )(*operands)


def per_device(
    seqs, tps, tokens, grad_out, qkv_weight, out_weight, mod_shift, mod_scale, mod_gate
):
    width = tokens.shape[-1]
    patches = tokens.shape[0] // seqs
    chunks = max(1, patches // 8)
    part = patches // chunks
    dims = (chunks, seqs, part, width)
    array = jax.ShapeDtypeStruct(dims, BF16)
    weights = jnp.transpose(qkv_weight, (0, 2, 1, 3))
    x = tokens.reshape(seqs, chunks, part, width).transpose(1, 0, 2, 3)
    g = grad_out.reshape(chunks, part, seqs, width).transpose(0, 2, 1, 3)

    cached = jax.ShapeDtypeStruct((3, tokens.shape[0], out_weight.shape[1]), BF16)
    part_s, qkv_s = compute(
        spatial_forward, (array, cached), x, mod_shift, mod_scale, weights, out_weight
    )
    mid = exchange(middle_kernel, 0, array, 1, True, seqs, tps, 4, part_s, x, mod_gate)
    part_t, gpart_t = compute(
        temporal, (array, array),
        mid, g, mod_shift, mod_scale, mod_gate, weights, out_weight,
    )
    result, grad_mid = exchange(
        temporal_sums, 1, (array, array), 2, True, seqs, tps, 2,
        gpart_t, part_t, mid, g, mod_gate, mod_scale,
    )
    gpart_s = compute(spatial_backward, array, grad_mid, mod_gate, weights, out_weight, qkv_s)
    grad_in = exchange(
        spatial_sums, 2, array, 1, False, seqs, tps, 4, gpart_s, x, grad_mid, mod_scale
    )
    result = result.transpose(0, 2, 1, 3).reshape(grad_out.shape)
    return (result, grad_in.transpose(1, 0, 2, 3).reshape(tokens.shape))


def solution(mesh):
    in_specs = (
        P(None, "seq", None),
        P("seq", None, None),
        P(None, None, None, "tp"),
        P(None, "tp", None),
        P(),
        P(),
        P(),
    )
    out_specs = (P("seq", None, None), P(None, "seq", None))
    return jax.shard_map(
        functools.partial(per_device, mesh.shape["seq"], mesh.shape["tp"]),
        mesh=mesh,
        in_specs=in_specs,
        out_specs=out_specs,
        check_vma=False,
    )
```

```python
import functools
import math

import jax
import jax.numpy as jnp
from jax import lax
from jax.experimental import pallas as pl
from jax.experimental.pallas import tpu as pltpu
from jax.sharding import PartitionSpec as P

HEAD_DIM = 72
BF16 = jnp.bfloat16
F32 = jnp.float32
MESH = pl.DeviceIdType.MESH
VMEM = pl.BlockSpec(memory_space=pltpu.VMEM)
LIMIT = 28 * 1024 * 1024


def dot_nn(a, b):
    return lax.dot_general(a, b, (((1,), (0,)), ((), ())), preferred_element_type=F32)


def dot_nt(a, b):
    return lax.dot_general(a, b, (((1,), (1,)), ((), ())), preferred_element_type=F32)


def dot_tn(a, b):
    return lax.dot_general(a, b, (((0,), (0,)), ((), ())), preferred_element_type=F32)


def normalize(rows):
    widened = rows.astype(F32)
    center = widened - jnp.mean(widened, axis=-1, keepdims=True)
    inv_std = lax.rsqrt(jnp.mean(center * center, axis=-1, keepdims=True) + 1e-06)
    return center * inv_std, inv_std


def project(rows, shift_ref, scale_ref, weight_ref, b):
    normed, _ = normalize(rows)
    modded = (normed * (1.0 + scale_ref[b : b + 1]) + shift_ref[b : b + 1]).astype(BF16)
    return tuple(dot_nn(modded, weight_ref[b, c]).astype(BF16) for c in range(3))


def head_masks(width):
    lane = lax.broadcasted_iota(jnp.int32, (1, width), 1)
    return [
        (lane >= h * HEAD_DIM) & (lane < (h + 1) * HEAD_DIM) for h in range(width // HEAD_DIM)
    ]


def pick(mask, value):
    return jnp.where(mask, value, jnp.zeros_like(value))


def head_probs(queries, keys, mask, same):
    scores = dot_nt(pick(mask, queries), keys) * (1.0 / math.sqrt(HEAD_DIM))
    if same is not None:
        scores = jnp.where(same, scores, -jnp.inf)
    shifted = jnp.exp(scores - jnp.max(scores, axis=-1, keepdims=True))
    return shifted / jnp.sum(shifted, axis=-1, keepdims=True)


def same_patch(total, seqs, part):
    row = lax.broadcasted_iota(jnp.int32, (total, total), 0)
    col = lax.broadcasted_iota(jnp.int32, (total, total), 1)
    block = seqs * part
    return (row // block == col // block) & (row % part == col % part)


def backward_heads(queries, keys, values, grad_attn, probs_of):
    masks = head_masks(queries.shape[1])
    grads = [jnp.zeros(queries.shape, F32) for _ in range(3)]
    for h, mask in enumerate(masks):
        probs = probs_of(h, mask)
        grad_probs = dot_nt(pick(mask, grad_attn), values)
        mean = jnp.sum(probs * grad_probs, axis=-1, keepdims=True)
        grad_scores = (probs * (grad_probs - mean) * (1.0 / math.sqrt(HEAD_DIM))).astype(BF16)
        grads[0] = jnp.where(mask, dot_nn(grad_scores, keys), grads[0])
        grads[1] = jnp.where(mask, dot_tn(grad_scores, queries), grads[1])
        grads[2] = jnp.where(mask, dot_tn(probs.astype(BF16), grad_attn), grads[2])
    return [grad.astype(BF16) for grad in grads]


def back_project(grads, weight_ref, b):
    total = dot_nt(grads[0], weight_ref[b, 0])
    total += dot_nt(grads[1], weight_ref[b, 1])
    return total + dot_nt(grads[2], weight_ref[b, 2])


def as_rows(ref):
    return ref[...].astype(F32).reshape(-1, ref.shape[-1])


def put(ref, value):
    ref[...] = value.reshape(ref.shape).astype(BF16)


def spatial_forward(x_ref, shift_ref, scale_ref, weight_ref, out_ref, part_ref, qkv_ref):
    queries, keys, values = project(as_rows(x_ref), shift_ref, scale_ref, weight_ref, 0)
    attended = jnp.zeros(queries.shape, F32)
    for mask in head_masks(queries.shape[1]):
        probs = head_probs(queries, keys, mask, None).astype(BF16)
        attended = jnp.where(mask, dot_nn(probs, values), attended)
    put(part_ref, dot_nn(attended.astype(BF16), out_ref[0]))
    for c, item in enumerate((queries, keys, values)):
        qkv_ref[c] = item


def grad_of_attended(g_ref, gate_ref, out_ref, b):
    grad_proj = (gate_ref[b : b + 1] * as_rows(g_ref)).astype(BF16)
    return dot_nt(grad_proj, out_ref[b]).astype(BF16)


def spatial_backward(g_ref, gate_ref, weight_ref, out_ref, qkv_ref, part_ref):
    queries, keys, values = (qkv_ref[c] for c in range(3))
    grad_attn = grad_of_attended(g_ref, gate_ref, out_ref, 0)
    grads = backward_heads(
        queries, keys, values, grad_attn, lambda h, mask: head_probs(queries, keys, mask, None)
    )
    put(part_ref, back_project(grads, weight_ref, 0))


def temporal(
    x_ref, g_ref, shift_ref, scale_ref, gate_ref, weight_ref, out_ref, part_ref, gpart_ref
):
    _, seqs, part, _ = x_ref.shape
    queries, keys, values = project(as_rows(x_ref), shift_ref, scale_ref, weight_ref, 1)
    same = same_patch(queries.shape[0], seqs, part)
    grad_attn = grad_of_attended(g_ref, gate_ref, out_ref, 1)
    probs = []
    attended = jnp.zeros(queries.shape, F32)
    for mask in head_masks(queries.shape[1]):
        probs.append(head_probs(queries, keys, mask, same))
        attended = jnp.where(mask, dot_nn(probs[-1].astype(BF16), values), attended)
    put(part_ref, dot_nn(attended.astype(BF16), out_ref[1]))
    grads = backward_heads(queries, keys, values, grad_attn, lambda h, mask: probs[h])
    put(gpart_ref, back_project(grads, weight_ref, 1))


def forward_end(total, x_ref, piece, gate_ref, b):
    return (x_ref[piece].astype(F32) + gate_ref[b : b + 1] * total).astype(BF16)


def backward_end(total, x_ref, piece, g_ref, scale_ref, b):
    normed, inv_std = normalize(x_ref[piece])
    grad_norm = total * (1.0 + scale_ref[b : b + 1])
    back = inv_std * (
        grad_norm
        - jnp.mean(grad_norm, axis=-1, keepdims=True)
        - normed * jnp.mean(grad_norm * normed, axis=-1, keepdims=True)
    )
    return (g_ref[piece].astype(F32) + back).astype(BF16)


def head_sums(parts, totals, ends, moved, scratch, seqs, tps, splits):
    inbox, halves, others, sems, seq_sems, own_sem = scratch
    s, z = lax.axis_index("seq"), lax.axis_index("tp")
    chunks = parts[0].shape[0]
    inner = (z > 0) & (z < tps - 1)
    outer = jnp.logical_not(inner)
    near = jnp.where(z < tps // 2, z + 1, z - 1)
    far = jnp.where(z < tps // 2, z - 1, z + 1)
    across = near
    barrier = pltpu.get_barrier_semaphore()

    def greet(tp):
        pl.semaphore_signal(barrier, inc=1, device_id=(s, tp), device_id_type=MESH)

    greet(near)

    @pl.when(inner)
    def _():
        greet(far)

    any_moved = any(item is not None for item in moved)
    if any_moved:

        @pl.loop(1, seqs)
        def _(k):
            pl.semaphore_signal(
                barrier, inc=1, device_id=(lax.rem(s + k, seqs), z), device_id_type=MESH
            )

    peers = seqs - 1 if any_moved else 0

    @pl.when(inner)
    def _():
        pl.semaphore_wait(barrier, 2 + peers)

    @pl.when(outer)
    def _():
        pl.semaphore_wait(barrier, 1 + peers)

    step = seqs // splits
    items = [(i, k) for k in range(chunks * splits) for i in range(len(parts))]

    def piece_of(k):
        return k // splits, pl.ds(k % splits * step, step)

    def remote(src, dst, kind, i, k, tp):
        return pltpu.make_async_remote_copy(
            src_ref=src.at[piece_of(k)],
            dst_ref=dst.at[piece_of(k)],
            send_sem=sems.at[kind, 0, i, k],
            recv_sem=sems.at[kind, 1, i, k],
            device_id=(s, tp),
            device_id_type=MESH,
        )

    def inward(i, c):
        return remote(parts[i], inbox.at[i], 0, i, c, near)

    def cross(i, c):
        return remote(halves.at[i], others.at[i], 1, i, c, across)

    def outward(i, c):
        return remote(totals[i], totals[i], 2, i, c, far)

    def spread(i, k):
        c, first = k // splits, k % splits * step

        @pl.loop(first, first + step)
        def _(to):
            @pl.when(to != s)
            def _():
                pltpu.make_async_remote_copy(
                    src_ref=totals[i].at[c, to],
                    dst_ref=moved[i].at[c, s],
                    send_sem=seq_sems.at[0, c],
                    recv_sem=seq_sems.at[1, c],
                    device_id=(to, z),
                    device_id_type=MESH,
                ).start()

            @pl.when(to == s)
            def _():
                pltpu.make_async_copy(
                    totals[i].at[c, s], moved[i].at[c, s], own_sem.at[c]
                ).start()

    count = len(items)

    @pl.when(outer)
    def _():
        flight, lead = 4, 6
        for at in range(count + lead):
            if at < count:
                if at >= flight:
                    inward(*items[at - flight]).wait_send()
                inward(*items[at]).start()
            if at >= lead:
                i, k = items[at - lead]
                outward(i, k).wait_recv()
                if moved[i] is not None:
                    spread(i, k)
        for item in items[count - flight :]:
            inward(*item).wait_send()

    @pl.when(inner)
    def _():
        def fold(i, k):
            inward(i, k).wait_recv()
            at = (i, *piece_of(k))
            halves[at] = (parts[i][at[1:]].astype(F32) + inbox[at].astype(F32)).astype(BF16)
            cross(i, k).start()

        def finish(i, k):
            cross(i, k).wait_recv()
            at = (i, *piece_of(k))
            total = halves[at].astype(F32) + others[at].astype(F32)
            totals[i][at[1:]] = ends[i](total, at[1:])
            outward(i, k).start()
            if moved[i] is not None:
                spread(i, k)

        lead = 3
        for at in range(count + lead):
            if at < count:
                fold(*items[at])
            if at >= lead:
                finish(*items[at - lead])
        for i, k in items:
            cross(i, k).wait_send()
            outward(i, k).wait_send()

    for i, c in [(i, c) for c in range(chunks) for i in range(len(parts))]:
        if moved[i] is not None:
            pltpu.make_async_copy(totals[i].at[c, s], moved[i].at[c, s], own_sem.at[c]).wait()
            rest = pl.ds(0, seqs - 1)
            both = pltpu.make_async_remote_copy(
                src_ref=totals[i].at[c, rest],
                dst_ref=moved[i].at[c, rest],
                send_sem=seq_sems.at[0, c],
                recv_sem=seq_sems.at[1, c],
                device_id=(lax.rem(s + 1, seqs), z),
                device_id_type=MESH,
            )
            both.wait_send()
            both.wait_recv()


def middle_kernel(seqs, tps, splits, part_ref, x_ref, gate_ref, mid_ref, total, *scratch):
    ends = [lambda value, at: forward_end(value, x_ref, at, gate_ref, 0)]
    head_sums([part_ref], [total], ends, [mid_ref], scratch, seqs, tps, splits)


def temporal_sums(
    seqs, tps, splits, gpart_ref, part_ref, x_ref, g_ref, gate_ref, scale_ref, result_ref, back_ref,
    total, *scratch
):
    ends = [
        lambda value, at: backward_end(value, x_ref, at, g_ref, scale_ref, 1),
        lambda value, at: forward_end(value, x_ref, at, gate_ref, 1),
    ]
    head_sums(
        [gpart_ref, part_ref], [total, result_ref], ends, [back_ref, None],
        scratch, seqs, tps, splits,
    )


def spatial_sums(seqs, tps, splits, gpart_ref, x_ref, g_ref, scale_ref, grad_ref, *scratch):
    ends = [lambda value, at: backward_end(value, x_ref, at, g_ref, scale_ref, 0)]
    head_sums([gpart_ref], [grad_ref], ends, [None], scratch, seqs, tps, splits)


def compute(body, outs, *operands):
    return pl.pallas_call(
        body,
        out_shape=outs,
        in_specs=[VMEM] * len(operands),
        out_specs=jax.tree.map(lambda _: VMEM, outs),
        compiler_params=pltpu.CompilerParams(vmem_limit_bytes=LIMIT),
    )(*operands)


def exchange(body, ident, outs, streams, own_total, seqs, tps, splits, *operands):
    shape = operands[0].shape
    chunks = shape[0]
    splits = math.gcd(seqs, splits)
    scratch = [pltpu.VMEM(shape, BF16)] if own_total else []
    scratch += [pltpu.VMEM((streams, *shape), BF16)] * 3
    scratch += [
        pltpu.SemaphoreType.DMA((3, 2, streams, chunks * splits)),
        pltpu.SemaphoreType.DMA((2, chunks)),
        pltpu.SemaphoreType.DMA((chunks,)),
    ]
    return pl.pallas_call(
        functools.partial(body, seqs, tps, splits),
        out_shape=outs,
        in_specs=[VMEM] * len(operands),
        out_specs=jax.tree.map(lambda _: VMEM, outs),
        scratch_shapes=scratch,
        compiler_params=pltpu.CompilerParams(
            collective_id=ident, has_side_effects=True, vmem_limit_bytes=LIMIT
        ),
    )(*operands)


def per_device(
    seqs, tps, tokens, grad_out, qkv_weight, out_weight, mod_shift, mod_scale, mod_gate
):
    width = tokens.shape[-1]
    patches = tokens.shape[0] // seqs
    chunks = max(1, patches // 8)
    part = patches // chunks
    dims = (chunks, seqs, part, width)
    array = jax.ShapeDtypeStruct(dims, BF16)
    weights = jnp.transpose(qkv_weight, (0, 2, 1, 3))
    x = tokens.reshape(seqs, chunks, part, width).transpose(1, 0, 2, 3)
    g = grad_out.reshape(chunks, part, seqs, width).transpose(0, 2, 1, 3)

    cached = jax.ShapeDtypeStruct((3, tokens.shape[0], out_weight.shape[1]), BF16)
    part_s, qkv_s = compute(
        spatial_forward, (array, cached), x, mod_shift, mod_scale, weights, out_weight
    )
    mid = exchange(middle_kernel, 0, array, 1, True, seqs, tps, 2, part_s, x, mod_gate)
    part_t, gpart_t = compute(
        temporal, (array, array),
        mid, g, mod_shift, mod_scale, mod_gate, weights, out_weight,
    )
    result, grad_mid = exchange(
        temporal_sums, 1, (array, array), 2, True, seqs, tps, 2,
        gpart_t, part_t, mid, g, mod_gate, mod_scale,
    )
    gpart_s = compute(spatial_backward, array, grad_mid, mod_gate, weights, out_weight, qkv_s)
    grad_in = exchange(
        spatial_sums, 2, array, 1, False, seqs, tps, 2, gpart_s, x, grad_mid, mod_scale
    )
    result = result.transpose(0, 2, 1, 3).reshape(grad_out.shape)
    return (result, grad_in.transpose(1, 0, 2, 3).reshape(tokens.shape))


def solution(mesh):
    in_specs = (
        P(None, "seq", None),
        P("seq", None, None),
        P(None, None, None, "tp"),
        P(None, "tp", None),
        P(),
        P(),
        P(),
    )
    out_specs = (P("seq", None, None), P(None, "seq", None))
    return jax.shard_map(
        functools.partial(per_device, mesh.shape["seq"], mesh.shape["tp"]),
        mesh=mesh,
        in_specs=in_specs,
        out_specs=out_specs,
        check_vma=False,
    )
```
